32 devices in a mesh: groups: 2 (over x), face: 8 (over z, y), tile: 2 (over core).
Axes of the slice: x: 2, y: 2, z: 4, core: 2. Of those that a mesh axis runs over, the one named last changes fastest.
Arguments:
- fields: float32 [32, 64, 128, 128], P(('groups', 'face'), None, 'tile'), parts along dimension 0, may hold values from -8 to 8
- cotangent: float32 [32, 64, 128, 128], P(('groups', 'face'), None, 'tile'), parts along dimension 0, may hold values from -0.125 to 0.125
- first_kernel: float32 [64, 64, 3, 3], replicated, may hold values from -0.25 to 0.25
- second_kernel: float32 [64, 64, 3, 3], replicated, may hold values from -0.25 to 0.25
- coarse_kernel: float32 [64, 64, 3, 3], replicated, may hold values from -0.25 to 0.25
- slot_faces: int32 [16], replicated, may hold values from -1 to 11, as said below
- edge_table: int32 [16, 4, 2], replicated, may hold values from 0 to 15, as said below
- corner_table: int32 [16, 4, 3], replicated, may hold values from 0 to 15, as said below
Outputs:
- section_output: float32 [32, 64, 128, 128], P(('groups', 'face'), None, 'tile'), parts along dimension 0
- grad_first: float32 [128, 64, 3, 3], P('groups'), parts along dimension 0
- grad_second: float32 [128, 64, 3, 3], P('groups'), parts along dimension 0
- grad_coarse: float32 [128, 64, 3, 3], P('groups'), parts along dimension 0
The draws below stay inside these ranges and needn't reach their ends.
There are 2 independent parts, one for each index of `groups`. The reference program is written for one: setup_inputs(seed, part) draws one part's arguments, and reference() takes and returns one part's arrays. A program takes and returns all parts, laid end to end along the dimension named above; an argument that names none is the same for every part. Nothing has to cross between parts.
Inputs may be any that keep to these rules, and one draw needn't show every extreme that they name: `slot_faces`: each face 0 to 11 stands in exactly one slot; the other slots hold -1. `edge_table`: for an occupied slot the entries follow the HEALPix base tessellation under the slot map; an empty slot names itself and its own side. The relation is symmetric: if side s of slot q names side t of slot p, then side t of p names side s of q. `corner_table`: entry [q, k, 2] is 1 where a fourth face meets diagonally at corner k, else 0 and the entry names slot q and corner k itself; empty slots name themselves. The relation is symmetric: if corner k of q names corner m of p, then corner m of p names corner k of q.
All inputs are finite; a program needn't handle non-finite values.
Results may differ from the reference program's by a relative error of at most 0.0003.
Values sent between devices are 32-bit elements; how exact they have to be, the bound alone decides.
A program may use at most 256 MiB of HBM per device.

```python
import math
from functools import partial
import jax
import jax.numpy as jnp
import numpy as np
from jax import lax

C = 64
NSIDE = 128
BLOCK = 4
FACES = 12
SLOTS = 16


edge_faces = np.array([[5, 1, 3, 4], [6, 2, 0, 5], [7, 3, 1, 6], [4, 0, 2, 7], [8, 0, 3, 11], [9, 1, 0, 8], [10, 2, 1, 9], [11, 3, 2, 10], [9, 5, 4, 11], [10, 6, 5, 8], [11, 7, 6, 9], [8, 4, 7, 10]], np.int32)


edge_sides = np.array([[2, 2, 1, 1]] * 4 + [[2, 3, 0, 1]] * 4 + [[3, 3, 0, 0]] * 4, np.int32)


corner_faces = np.array([[8, 0, 2, 0], [9, 1, 3, 1], [10, 2, 0, 2], [11, 3, 1, 3], [4, 5, 4, 7], [5, 6, 5, 4], [6, 7, 6, 5], [7, 4, 7, 6], [10, 8, 0, 8], [11, 9, 1, 9], [8, 10, 2, 10], [9, 11, 3, 11]], np.int32)


corner_which = np.array([[2, 1, 2, 3]] * 4 + [[0, 3, 2, 1]] * 4 + [[0, 1, 0, 3]] * 4, np.int32)


corner_flags = np.array([[1, 0, 1, 0]] * 4 + [[0, 1, 0, 1]] * 4 + [[1, 0, 1, 0]] * 4, np.int32)


def face_slots(key):
    return jax.random.permutation(jax.random.fold_in(key, 17), SLOTS)[:FACES].astype(jnp.int32)


def draw_slot_faces(key, part):
    placed = face_slots(key)
    return jnp.full((SLOTS,), -1, jnp.int32).at[placed].set(jnp.arange(FACES, dtype=jnp.int32))


def draw_edge_table(key, part):
    placed = face_slots(key)
    itself = jnp.broadcast_to(jnp.arange(SLOTS, dtype=jnp.int32)[:, None], (SLOTS, 4))
    side_ids = jnp.broadcast_to(jnp.arange(4, dtype=jnp.int32)[None, :], (SLOTS, 4))
    base_table = jnp.stack([itself, side_ids], axis=-1)
    filled = jnp.stack([placed[jnp.asarray(edge_faces)], jnp.asarray(edge_sides)], axis=-1)
    return base_table.at[placed].set(filled)


def draw_corner_table(key, part):
    placed = face_slots(key)
    itself = jnp.broadcast_to(jnp.arange(SLOTS, dtype=jnp.int32)[:, None], (SLOTS, 4))
    corner_ids = jnp.broadcast_to(jnp.arange(4, dtype=jnp.int32)[None, :], (SLOTS, 4))
    base_table = jnp.stack([itself, corner_ids, jnp.zeros((SLOTS, 4), jnp.int32)], axis=-1)
    filled = jnp.stack([placed[jnp.asarray(corner_faces)], jnp.asarray(corner_which), jnp.asarray(corner_flags)], axis=-1)
    return base_table.at[placed].set(filled)


def draw_fields(key, part):
    subkeys = jax.random.split(key, 7)
    full_shape = (SLOTS, C, NSIDE, NSIDE)
    noise_part = jax.random.normal(subkeys[0], full_shape, jnp.float32)
    offsets = 0.6 * jax.random.normal(subkeys[2], (SLOTS, C, 1, 1), jnp.float32)
    amplitude = jax.random.uniform(subkeys[3], (SLOTS, C, 1, 1), jnp.float32, 0.2, 1.0)
    freq_rows = jax.random.randint(subkeys[4], (SLOTS, 1, 1, 1), 1, 4).astype(jnp.float32)
    freq_cols = jax.random.randint(subkeys[5], (SLOTS, 1, 1, 1), 1, 4).astype(jnp.float32)
    phases = jax.random.uniform(subkeys[6], (SLOTS, C, 1, 1), jnp.float32, 0.0, 2.0 * math.pi)
    position = jnp.arange(NSIDE, dtype=jnp.float32) / NSIDE
    pattern = amplitude * jnp.cos(2.0 * math.pi * (freq_rows * position[:, None] + freq_cols * position[None, :]) + phases)
    return jnp.clip(noise_part + offsets + pattern, -8.0, 8.0)


def levels(rng, extent, cuts, least, high):
    level = 1.0
    for dim, blocks in cuts:
        draws = jax.random.uniform(jax.random.fold_in(jax.random.fold_in(rng, 6), dim), (blocks,), jnp.float32, least / len(cuts), high / len(cuts))
        level = level * jnp.repeat(jnp.exp(draws), extent[dim] // blocks).reshape((-1,) + (1,) * (len(extent) - 1 - dim))
    return level


def bell_draw(own_key, dims, deviation, reach, shards=(), kind=jnp.bfloat16):
    loudness = levels(own_key, dims, shards, -0.22, 0.18) if shards else 1.0
    values = jax.random.normal(own_key, dims, jnp.float32) * deviation * loudness
    return jnp.minimum(jnp.maximum(values, -reach), reach).astype(kind)


def setup_inputs(seed: int = 0, part: int = 0) -> dict:
    keys = jax.random.split(jax.random.key(seed), 9)
    part_splits = jax.random.split(jax.random.fold_in(keys[8], part), 9)
    return {
        "fields": draw_fields(jax.random.fold_in(jax.random.fold_in(keys[8], part), 71), part),
        "cotangent": bell_draw(part_splits[1], (SLOTS, C, NSIDE, NSIDE), (1.0 / NSIDE), 0.125, ((0, 8), (2, 2)), jnp.float32),
        "first_kernel": bell_draw(keys[2], (C, C, 3, 3), (9 * C) ** -0.5, 0.25, (), jnp.float32),
        "second_kernel": bell_draw(keys[3], (C, C, 3, 3), (9 * C) ** -0.5, 0.25, (), jnp.float32),
        "coarse_kernel": bell_draw(keys[4], (C, C, 3, 3), (9 * C) ** -0.5, 0.25, (), jnp.float32),
        "slot_faces": draw_slot_faces(jax.random.fold_in(keys[8], 71), part),
        "edge_table": draw_edge_table(jax.random.fold_in(keys[8], 71), part),
        "corner_table": draw_corner_table(jax.random.fold_in(keys[8], 71), part),
    }


def convolve(padded, kernel):
    return lax.conv_general_dilated(padded, kernel, (1, 1), 'VALID', precision=lax.Precision.HIGHEST)

def activate(values):
    return jax.nn.gelu(values, approximate=False)

def corner_values(halo_lines, picked, flags):
    south_east = halo_lines[:, 0]
    north_east = halo_lines[:, 1]
    north_west = halo_lines[:, 2]
    south_west = halo_lines[:, 3]
    averaged = jnp.stack([0.5 * (south_east[..., 0] + south_west[..., 0]), 0.5 * (south_east[..., -1] + north_east[..., 0]), 0.5 * (north_west[..., -1] + north_east[..., -1]), 0.5 * (north_west[..., 0] + south_west[..., -1])], axis=1)
    return jnp.where((flags == 1)[:, :, None], picked, averaged)

def frame_field(fields, halo_lines, corners):
    west_line = jnp.concatenate([corners[:, 0, :, None], halo_lines[:, 3], corners[:, 3, :, None]], axis=-1)
    east_line = jnp.concatenate([corners[:, 1, :, None], halo_lines[:, 1], corners[:, 2, :, None]], axis=-1)
    top_row = jnp.concatenate([west_line[..., :1], halo_lines[:, 0], east_line[..., :1]], axis=-1)
    bottom = jnp.concatenate([west_line[..., -1:], halo_lines[:, 2], east_line[..., -1:]], axis=-1)
    middle = jnp.concatenate([west_line[..., 1:-1, None], fields, east_line[..., 1:-1, None]], axis=-1)
    return jnp.concatenate([top_row[:, :, None], middle, bottom[:, :, None]], axis=2)

def pad_faces(fields, edge_table, corner_table):
    last_index = fields.shape[-1] - 1
    rim_lines = jnp.stack([fields[:, :, 0, :], fields[:, :, :, last_index], fields[:, :, last_index, :], fields[:, :, :, 0]], axis=1)
    halo_lines = rim_lines[edge_table[:, :, 0], edge_table[:, :, 1]]
    corner_cells = jnp.stack([fields[:, :, 0, 0], fields[:, :, 0, last_index], fields[:, :, last_index, last_index], fields[:, :, last_index, 0]], axis=1)
    picked = corner_cells[corner_table[:, :, 0], corner_table[:, :, 1]]
    return frame_field(fields, halo_lines, corner_values(halo_lines, picked, corner_table[:, :, 2]))

def pooled(values):
    return values.reshape(values.shape[0], values.shape[1], values.shape[2] // BLOCK, BLOCK, values.shape[3] // BLOCK, BLOCK).mean(axis=(3, 5))

def reference(fields, cotangent, first_kernel, second_kernel, coarse_kernel, slot_faces, edge_table, corner_table):
    occupied = (slot_faces >= 0).astype(jnp.float32)[:, None, None, None]
    padding = partial(pad_faces, edge_table=edge_table, corner_table=corner_table)

    def forward(kernel_one, kernel_two, kernel_low):
        hidden = activate(convolve(padding(fields), kernel_one))
        features = activate(convolve(padding(hidden), kernel_two))
        bottleneck = activate(convolve(padding(pooled(features)), kernel_low))
        widened = jnp.repeat(jnp.repeat(bottleneck, BLOCK, axis=2), BLOCK, axis=3)
        return (features + widened) * occupied
    section_output, pullback = jax.vjp(forward, first_kernel, second_kernel, coarse_kernel)
    grad_first, grad_second, grad_coarse = pullback(cotangent)
    return (section_output, grad_first, grad_second, grad_coarse)
```

```python
from functools import partial

import jax
import jax.numpy as jnp
from jax import lax
from jax.sharding import PartitionSpec as P

BLOCK = 4


def convolve(padded, kernel):
    return lax.conv_general_dilated(
        padded, kernel, (1, 1), "VALID", precision=lax.Precision.HIGH
    )


def activate(values):
    return jax.nn.gelu(values, approximate=False)


def rim_pieces(tile_field):
    last_row = tile_field.shape[2] - 1
    last_col = tile_field.shape[3] - 1
    columns = jnp.stack([tile_field[:, :, :, 0], tile_field[:, :, :, last_col]], axis=1)[None]
    borders = jnp.stack([tile_field[:, :, 0, :], tile_field[:, :, last_row, :]], axis=1)[None]
    return (columns, borders)


def fine_gather(tile_field):
    columns, borders = rim_pieces(tile_field)
    tile_rows = columns.shape[-1]
    both = lax.all_gather(
        jnp.concatenate([columns, borders], axis=-1), ("face", "tile"), axis=0, tiled=True
    )
    return (both[..., :tile_rows], both[..., tile_rows:])


def fine_return(grad_columns, grad_borders):
    tile_rows = grad_columns.shape[-1]
    both = lax.psum_scatter(
        jnp.concatenate([grad_columns, grad_borders], axis=-1),
        ("face", "tile"),
        scatter_dimension=0,
        tiled=True,
    )
    return (both[..., :tile_rows], both[..., tile_rows:])


def fetch_lines(
    columns_all, borders_all, face_index, tile_index, face_count, tile_count, my_edges, my_corners
):
    slots_dev = columns_all.shape[1]
    channels = columns_all.shape[3]
    tile_rows = columns_all.shape[4]
    length = borders_all.shape[-1]
    cols_all = columns_all.reshape(face_count, tile_count, slots_dev, 2, channels, tile_rows)
    bord_all = borders_all.reshape(face_count, tile_count, slots_dev, 2, channels, length)
    near_slot = my_edges[:, :, 0]
    near_side = my_edges[:, :, 1]
    near_face = near_slot // slots_dev
    near_local = near_slot % slots_dev
    col_pick = jnp.where(near_side == 1, 1, 0)
    col_lines = cols_all[near_face, :, near_local, col_pick]
    col_lines = col_lines.transpose(0, 1, 3, 2, 4).reshape(
        slots_dev, 4, channels, tile_count * tile_rows
    )
    row_tile = jnp.where(near_side == 0, 0, tile_count - 1)
    row_pick = jnp.where(near_side == 0, 0, 1)
    row_lines = bord_all[near_face, row_tile, near_local, row_pick]
    halo_lines = jnp.where((near_side % 2 == 1)[:, :, None, None], col_lines, row_lines)
    corner_slot = my_corners[:, :, 0]
    corner_kind = my_corners[:, :, 1]
    corner_face = corner_slot // slots_dev
    corner_local = corner_slot % slots_dev
    corner_tile = jnp.where(corner_kind < 2, 0, tile_count - 1)
    corner_row = jnp.where(corner_kind < 2, 0, 1)
    corner_col = jnp.where((corner_kind == 0) | (corner_kind == 3), 0, length - 1)
    picked = bord_all[corner_face, corner_tile, corner_local, corner_row, :, corner_col]
    above_tile = bord_all[face_index, jnp.maximum(tile_index - 1, 0), :, 1]
    below_tile = bord_all[face_index, jnp.minimum(tile_index + 1, tile_count - 1), :, 0]
    return (halo_lines, picked, above_tile, below_tile)


def assemble(tile_field, pieces, tile_index, tile_count, my_corners):
    halo_lines, picked, above_tile, below_tile = pieces
    tile_rows = tile_field.shape[2]
    corner_flag = my_corners[:, :, 2]
    south_east = halo_lines[:, 0]
    north_east = halo_lines[:, 1]
    north_west = halo_lines[:, 2]
    south_west = halo_lines[:, 3]
    averaged = jnp.stack(
        [
            0.5 * (south_east[..., 0] + south_west[..., 0]),
            0.5 * (south_east[..., -1] + north_east[..., 0]),
            0.5 * (north_west[..., -1] + north_east[..., -1]),
            0.5 * (north_west[..., 0] + south_west[..., -1]),
        ],
        axis=1,
    )
    corners = jnp.where((corner_flag == 1)[:, :, None], picked, averaged)
    west_line = jnp.concatenate(
        [corners[:, 0, :, None], south_west, corners[:, 3, :, None]], axis=-1
    )
    east_line = jnp.concatenate(
        [corners[:, 1, :, None], north_east, corners[:, 2, :, None]], axis=-1
    )
    west_part = lax.dynamic_slice_in_dim(west_line, tile_index * tile_rows, tile_rows + 2, axis=2)
    east_part = lax.dynamic_slice_in_dim(east_line, tile_index * tile_rows, tile_rows + 2, axis=2)
    above_row = jnp.where(tile_index == 0, south_east, above_tile)
    below_row = jnp.where(tile_index == tile_count - 1, north_west, below_tile)
    top_row = jnp.concatenate([west_part[..., :1], above_row, east_part[..., :1]], axis=-1)
    bottom = jnp.concatenate([west_part[..., -1:], below_row, east_part[..., -1:]], axis=-1)
    middle = jnp.concatenate(
        [west_part[..., 1:-1, None], tile_field, east_part[..., 1:-1, None]], axis=-1
    )
    return jnp.concatenate([top_row[:, :, None], middle, bottom[:, :, None]], axis=2)


def framed_tile(
    tile_field,
    columns_all,
    borders_all,
    face_index,
    tile_index,
    face_count,
    tile_count,
    my_edges,
    my_corners,
):
    pieces = fetch_lines(
        columns_all,
        borders_all,
        face_index,
        tile_index,
        face_count,
        tile_count,
        my_edges,
        my_corners,
    )
    return assemble(tile_field, pieces, tile_index, tile_count, my_corners)


def local(
    fields,
    cotangent,
    first_kernel,
    second_kernel,
    coarse_kernel,
    slot_faces,
    edge_table,
    corner_table,
):
    face_index = lax.axis_index("face")
    tile_index = lax.axis_index("tile")
    face_count = lax.axis_size("face")
    tile_count = lax.axis_size("tile")
    slots_dev = fields.shape[0]
    my_slots = face_index * slots_dev + jnp.arange(slots_dev, dtype=jnp.int32)
    my_edges = edge_table[my_slots]
    my_corners = corner_table[my_slots]
    occupied = (slot_faces[my_slots] >= 0).astype(jnp.float32)[:, None, None, None]
    framer = partial(
        framed_tile,
        face_index=face_index,
        tile_index=tile_index,
        face_count=face_count,
        tile_count=tile_count,
        my_edges=my_edges,
        my_corners=my_corners,
    )
    columns_in, borders_in = fine_gather(fields)
    padded_in = framer(fields, columns_in, borders_in)
    first_act = convolve(padded_in, first_kernel)
    hidden, hidden_pull = jax.vjp(activate, first_act)
    columns_mid, borders_mid = fine_gather(hidden)
    padded_mid, frame_pull = jax.vjp(framer, hidden, columns_mid, borders_mid)
    second_act, second_pull = jax.vjp(convolve, padded_mid, second_kernel)
    features, features_pull = jax.vjp(activate, second_act)
    channels = features.shape[1]
    tile_rows = features.shape[2]
    length = features.shape[3]
    coarse = features.reshape(
        slots_dev, channels, tile_rows // BLOCK, BLOCK, length // BLOCK, BLOCK
    ).mean(axis=(3, 5))
    columns_low, borders_low = fine_gather(coarse)
    padded_low, low_pull = jax.vjp(framer, coarse, columns_low, borders_low)
    coarse_act, coarse_pull = jax.vjp(convolve, padded_low, coarse_kernel)
    bottleneck, bottleneck_pull = jax.vjp(activate, coarse_act)
    widened = jnp.repeat(jnp.repeat(bottleneck, BLOCK, axis=2), BLOCK, axis=3)
    section_output = (features + widened) * occupied
    masked = cotangent * occupied
    grad_bottleneck = masked.reshape(
        slots_dev, channels, tile_rows // BLOCK, BLOCK, length // BLOCK, BLOCK
    ).sum(axis=(3, 5))
    (grad_coarse_act,) = bottleneck_pull(grad_bottleneck)
    grad_padded_low, grad_coarse = coarse_pull(grad_coarse_act)
    grad_local, grad_columns_low, grad_borders_low = low_pull(grad_padded_low)
    back_low = fine_return(grad_columns_low, grad_borders_low)
    (spread_low,) = jax.vjp(rim_pieces, coarse)[1](back_low)
    grad_low = grad_local + spread_low
    grad_features = masked + jnp.repeat(jnp.repeat(grad_low, BLOCK, axis=2), BLOCK, axis=3) / (
        BLOCK * BLOCK
    )
    (grad_second_act,) = features_pull(grad_features)
    grad_padded_mid, grad_second = second_pull(grad_second_act)
    grad_hidden_local, grad_columns_mid, grad_borders_mid = frame_pull(grad_padded_mid)
    back_mid = fine_return(grad_columns_mid, grad_borders_mid)
    (spread_mid,) = jax.vjp(rim_pieces, hidden)[1](back_mid)
    grad_hidden = grad_hidden_local + spread_mid
    (grad_first_act,) = hidden_pull(grad_hidden)
    (grad_first,) = jax.vjp(partial(convolve, padded_in), first_kernel)[1](grad_first_act)
    grad_first, grad_second, grad_coarse = lax.psum(
        (grad_first, grad_second, grad_coarse), ("face", "tile")
    )
    return (section_output, grad_first, grad_second, grad_coarse)


def solution(mesh):
    in_specs = (
        P(("groups", "face"), None, "tile", None),
        P(("groups", "face"), None, "tile", None),
        P(),
        P(),
        P(),
        P(),
        P(),
        P(),
    )
    out_specs = (
        P(("groups", "face"), None, "tile", None),
        P("groups", None, None, None),
        P("groups", None, None, None),
        P("groups", None, None, None),
    )
    return jax.shard_map(local, mesh=mesh, in_specs=in_specs, out_specs=out_specs, check_vma=False)
```

```python
from functools import partial

import jax
import jax.numpy as jnp
from jax import lax
from jax.sharding import PartitionSpec as P

BLOCK = 4


def convolve(padded, kernel):
    return lax.conv_general_dilated(
        padded, kernel, (1, 1), "VALID", precision=lax.Precision.HIGH
    )


def activate(values):
    return jax.nn.gelu(values, approximate=False)


def activation_grad(values, grads):
    return jax.vjp(activate, lax.optimization_barrier(values))[1](grads)[0]


def split_sum(values, devices):
    turned = values.transpose(2, 3, 1, 0)
    shares = turned.reshape(devices, -1, 128)
    share = lax.psum_scatter(shares, ("face", "tile"), scatter_dimension=0, tiled=True)
    whole = lax.all_gather(share, ("face", "tile"), axis=0, tiled=True)
    return whole.reshape(turned.shape).transpose(3, 2, 0, 1)


def rim_pieces(tile_field):
    last_row = tile_field.shape[2] - 1
    last_col = tile_field.shape[3] - 1
    columns = jnp.stack([tile_field[:, :, :, 0], tile_field[:, :, :, last_col]], axis=1)[None]
    borders = jnp.stack([tile_field[:, :, 0, :], tile_field[:, :, last_row, :]], axis=1)[None]
    return (columns, borders)


def fine_gather(tile_field):
    columns, borders = rim_pieces(tile_field)
    tile_rows = columns.shape[-1]
    both = lax.all_gather(
        jnp.concatenate([columns, borders], axis=-1), ("face", "tile"), axis=0, tiled=True
    )
    return (both[..., :tile_rows], both[..., tile_rows:])


def fine_return(grad_columns, grad_borders):
    tile_rows = grad_columns.shape[-1]
    both = lax.psum_scatter(
        jnp.concatenate([grad_columns, grad_borders], axis=-1),
        ("face", "tile"),
        scatter_dimension=0,
        tiled=True,
    )
    return (both[..., :tile_rows], both[..., tile_rows:])


def fetch_lines(
    columns_all, borders_all, face_index, tile_index, face_count, tile_count, my_edges, my_corners
):
    slots_dev = columns_all.shape[1]
    channels = columns_all.shape[3]
    tile_rows = columns_all.shape[4]
    length = borders_all.shape[-1]
    cols_all = columns_all.reshape(face_count, tile_count, slots_dev, 2, channels, tile_rows)
    bord_all = borders_all.reshape(face_count, tile_count, slots_dev, 2, channels, length)
    near_slot = my_edges[:, :, 0]
    near_side = my_edges[:, :, 1]
    near_face = near_slot // slots_dev
    near_local = near_slot % slots_dev
    col_pick = jnp.where(near_side == 1, 1, 0)
    col_lines = cols_all[near_face, :, near_local, col_pick]
    col_lines = col_lines.transpose(0, 1, 3, 2, 4).reshape(
        slots_dev, 4, channels, tile_count * tile_rows
    )
    row_tile = jnp.where(near_side == 0, 0, tile_count - 1)
    row_pick = jnp.where(near_side == 0, 0, 1)
    row_lines = bord_all[near_face, row_tile, near_local, row_pick]
    halo_lines = jnp.where((near_side % 2 == 1)[:, :, None, None], col_lines, row_lines)
    corner_slot = my_corners[:, :, 0]
    corner_kind = my_corners[:, :, 1]
    corner_face = corner_slot // slots_dev
    corner_local = corner_slot % slots_dev
    corner_tile = jnp.where(corner_kind < 2, 0, tile_count - 1)
    corner_row = jnp.where(corner_kind < 2, 0, 1)
    corner_col = jnp.where((corner_kind == 0) | (corner_kind == 3), 0, length - 1)
    picked = bord_all[corner_face, corner_tile, corner_local, corner_row, :, corner_col]
    above_tile = bord_all[face_index, jnp.maximum(tile_index - 1, 0), :, 1]
    below_tile = bord_all[face_index, jnp.minimum(tile_index + 1, tile_count - 1), :, 0]
    return (halo_lines, picked, above_tile, below_tile)


def assemble(tile_field, pieces, tile_index, tile_count, my_corners):
    halo_lines, picked, above_tile, below_tile = pieces
    tile_rows = tile_field.shape[2]
    corner_flag = my_corners[:, :, 2]
    south_east = halo_lines[:, 0]
    north_east = halo_lines[:, 1]
    north_west = halo_lines[:, 2]
    south_west = halo_lines[:, 3]
    averaged = jnp.stack(
        [
            0.5 * (south_east[..., 0] + south_west[..., 0]),
            0.5 * (south_east[..., -1] + north_east[..., 0]),
            0.5 * (north_west[..., -1] + north_east[..., -1]),
            0.5 * (north_west[..., 0] + south_west[..., -1]),
        ],
        axis=1,
    )
    corners = jnp.where((corner_flag == 1)[:, :, None], picked, averaged)
    west_line = jnp.concatenate(
        [corners[:, 0, :, None], south_west, corners[:, 3, :, None]], axis=-1
    )
    east_line = jnp.concatenate(
        [corners[:, 1, :, None], north_east, corners[:, 2, :, None]], axis=-1
    )
    west_part = lax.dynamic_slice_in_dim(west_line, tile_index * tile_rows, tile_rows + 2, axis=2)
    east_part = lax.dynamic_slice_in_dim(east_line, tile_index * tile_rows, tile_rows + 2, axis=2)
    above_row = jnp.where(tile_index == 0, south_east, above_tile)
    below_row = jnp.where(tile_index == tile_count - 1, north_west, below_tile)
    top_row = jnp.concatenate([west_part[..., :1], above_row, east_part[..., :1]], axis=-1)
    bottom = jnp.concatenate([west_part[..., -1:], below_row, east_part[..., -1:]], axis=-1)
    middle = jnp.concatenate(
        [west_part[..., 1:-1, None], tile_field, east_part[..., 1:-1, None]], axis=-1
    )
    return jnp.concatenate([top_row[:, :, None], middle, bottom[:, :, None]], axis=2)


def framed_tile(
    tile_field,
    columns_all,
    borders_all,
    face_index,
    tile_index,
    face_count,
    tile_count,
    my_edges,
    my_corners,
):
    pieces = fetch_lines(
        columns_all,
        borders_all,
        face_index,
        tile_index,
        face_count,
        tile_count,
        my_edges,
        my_corners,
    )
    return assemble(tile_field, pieces, tile_index, tile_count, my_corners)


def local(
    fields,
    cotangent,
    first_kernel,
    second_kernel,
    coarse_kernel,
    slot_faces,
    edge_table,
    corner_table,
):
    face_index = lax.axis_index("face")
    tile_index = lax.axis_index("tile")
    face_count = lax.axis_size("face")
    tile_count = lax.axis_size("tile")
    slots_dev = fields.shape[0]
    my_slots = face_index * slots_dev + jnp.arange(slots_dev, dtype=jnp.int32)
    my_edges = edge_table[my_slots]
    my_corners = corner_table[my_slots]
    occupied = (slot_faces[my_slots] >= 0).astype(jnp.float32)[:, None, None, None]
    framer = partial(
        framed_tile,
        face_index=face_index,
        tile_index=tile_index,
        face_count=face_count,
        tile_count=tile_count,
        my_edges=my_edges,
        my_corners=my_corners,
    )
    columns_in, borders_in = fine_gather(fields)
    padded_in = framer(fields, columns_in, borders_in)
    first_act = convolve(padded_in, first_kernel)
    hidden = activate(first_act)
    columns_mid, borders_mid = fine_gather(hidden)
    padded_mid, frame_pull = jax.vjp(framer, hidden, columns_mid, borders_mid)
    second_act, second_pull = jax.vjp(convolve, padded_mid, second_kernel)
    features = activate(second_act)
    channels = features.shape[1]
    tile_rows = features.shape[2]
    length = features.shape[3]
    coarse = features.reshape(
        slots_dev, channels, tile_rows // BLOCK, BLOCK, length // BLOCK, BLOCK
    ).mean(axis=(3, 5))
    columns_low, borders_low = fine_gather(coarse)
    padded_low, low_pull = jax.vjp(framer, coarse, columns_low, borders_low)
    coarse_act, coarse_pull = jax.vjp(convolve, padded_low, coarse_kernel)
    bottleneck, bottleneck_pull = jax.vjp(activate, coarse_act)
    widened = jnp.repeat(jnp.repeat(bottleneck, BLOCK, axis=2), BLOCK, axis=3)
    section_output = (features + widened) * occupied
    masked = cotangent * occupied
    grad_bottleneck = masked.reshape(
        slots_dev, channels, tile_rows // BLOCK, BLOCK, length // BLOCK, BLOCK
    ).sum(axis=(3, 5))
    (grad_coarse_act,) = bottleneck_pull(grad_bottleneck)
    grad_padded_low, grad_coarse = coarse_pull(grad_coarse_act)
    grad_local, grad_columns_low, grad_borders_low = low_pull(grad_padded_low)
    back_low = fine_return(grad_columns_low, grad_borders_low)
    (spread_low,) = jax.vjp(rim_pieces, coarse)[1](back_low)
    grad_low = grad_local + spread_low
    grad_features = masked + jnp.repeat(jnp.repeat(grad_low, BLOCK, axis=2), BLOCK, axis=3) / (
        BLOCK * BLOCK
    )
    grad_second_act = activation_grad(second_act, grad_features)
    grad_padded_mid, grad_second = second_pull(grad_second_act)
    grad_hidden_local, grad_columns_mid, grad_borders_mid = frame_pull(grad_padded_mid)
    back_mid = fine_return(grad_columns_mid, grad_borders_mid)
    (spread_mid,) = jax.vjp(rim_pieces, hidden)[1](back_mid)
    grad_hidden = grad_hidden_local + spread_mid
    grad_second, grad_hidden = lax.optimization_barrier((grad_second, grad_hidden))
    grad_first_act = activation_grad(first_act, grad_hidden)
    (grad_first,) = jax.vjp(partial(convolve, padded_in), first_kernel)[1](grad_first_act)
    grad_second, grad_coarse = lax.psum((grad_second, grad_coarse), ("face", "tile"))
    grad_first = split_sum(grad_first, face_count * tile_count)
    return (section_output, grad_first, grad_second, grad_coarse)


def solution(mesh):
    in_specs = (
        P(("groups", "face"), None, "tile", None),
        P(("groups", "face"), None, "tile", None),
        P(),
        P(),
        P(),
        P(),
        P(),
        P(),
    )
    out_specs = (
        P(("groups", "face"), None, "tile", None),
        P("groups", None, None, None),
        P("groups", None, None, None),
        P("groups", None, None, None),
    )
    return jax.shard_map(local, mesh=mesh, in_specs=in_specs, out_specs=out_specs, check_vma=False)
```
